128 devices in a mesh: row: 16 (over y_hi, x, core), col: 8 (over z, y_lo).
Axes of the slice: x: 4, y: 4 (y_hi: 2, y_lo: 2; y = y_hi * 2 + y_lo), z: 4, core: 2. Of those that a mesh axis runs over, the one named last changes fastest.
Arguments:
- unsieved_electron_density: bfloat16 [8192, 8192], P('row', 'col')
- present_patch_indicator: int32 [64, 64], P('row', 'col'), may hold values 0 or 1
- surviving_patch_indicator: int32 [64, 64], P('row', 'col'), may hold values 0 or 1
- proprietor_rows: int32 [64, 64], P('row', 'col'), may hold values from 0 to 15, as said below
Outputs:
- delivered: bfloat16 [1024, 8, 16384], P('row', 'col')
The draws below stay inside these ranges and needn't reach their ends.
Inputs may be any that keep to these rules, and one draw needn't show every extreme that they name: `proprietor_rows`: the 4 x 8 blocks held by one device include at most 4 with the same owner. In each block-column group some owner receives 4 blocks from every device of the group.
All inputs are finite; a program needn't handle non-finite values. No bound on the sum of `present_patch_indicator` or of `surviving_patch_indicator` on one device may be relied on, other than what follows from the above.
Results may differ from the reference program's by a relative error of at most 0.0049.
Values may be sent and summed in bfloat16 or wider, within the bound.
A program may use at most 128 MiB of HBM per device.

```python
import jax
import jax.numpy as jnp

BLOCK = 128
RB = 4
CB = 8
TILES_ACROSS = 64
ORDER = 8192
SLOTS = 4
N_ROW = 16
N_COL = 8


def draw_unsieved_electron_density(key, part):
    key = jax.random.fold_in(key, 5)
    spread = (ORDER * 0.5) ** (-1.0 / 3.0)
    values = jax.random.normal(key, (ORDER, ORDER), jnp.float32) * spread
    return values.astype(jnp.bfloat16)


def draw_proprietor_rows(key, part):
    key = jax.random.fold_in(key, 11)
    per_holder_share = RB * CB
    half = per_holder_share // 2
    busy_count = N_ROW // 4
    other_count = N_ROW - busy_count
    extra_busy = max(busy_count - 1, 1)
    relabel = jax.random.permutation(key, N_ROW).astype(jnp.int32)
    rotation = jax.random.randint(jax.random.fold_in(key, 1), (N_ROW * N_COL,), 0, per_holder_share).astype(jnp.int32)
    column_shift = jax.random.randint(jax.random.fold_in(key, 2), (N_COL,), 0, N_ROW).astype(jnp.int32)
    rows_index = jnp.arange(TILES_ACROSS, dtype=jnp.int32)[:, None]
    cols_index = jnp.arange(TILES_ACROSS, dtype=jnp.int32)[None, :]
    source_row = rows_index // RB
    source_col = cols_index // CB
    source = source_row * N_COL + source_col
    within = rows_index % RB * CB + cols_index % CB
    turned = (within + rotation[source]) % per_holder_share
    group = turned // SLOTS
    busy_rank = jnp.where(group == 0, 0, 1 + (group - 1 + source_row) % extra_busy)
    other_rank = busy_count + (source_row + turned - half) % other_count
    rank = jnp.where(turned < half, busy_rank, other_rank)
    return relabel[(rank + column_shift[source_col]) % N_ROW].astype(jnp.int32)


def set_ends(drawn, stream_key, low, largest):
    extent = drawn.shape
    index_at = [jax.random.randint(jax.random.fold_in(stream_key, axis), (), 0, extent[axis]) for axis in range(len(extent))]
    drawn = drawn.at[tuple(index_at)].set(low)
    longest = extent.index(max(extent))
    index_at[longest] = (index_at[longest] + 1) % extent[longest]
    return drawn.at[tuple(index_at)].set(largest)


def setup_inputs(seed: int = 0) -> dict:
    keys = jax.random.split(jax.random.key(seed), 5)
    unsieved_electron_density = draw_unsieved_electron_density(jax.random.fold_in(keys[4], 71), 0)
    present_patch_indicator = set_ends((jax.random.randint(keys[1], (TILES_ACROSS, TILES_ACROSS), 0, 2) < 1).astype(jnp.int32), jax.random.fold_in(keys[1], 1), 0, 1)
    surviving_patch_indicator = set_ends((jax.random.randint(keys[2], (TILES_ACROSS, TILES_ACROSS), 0, 4) < 3).astype(jnp.int32), jax.random.fold_in(keys[2], 1), 0, 1)
    proprietor_rows = draw_proprietor_rows(jax.random.fold_in(keys[4], 71), 0)
    return {"unsieved_electron_density": unsieved_electron_density, "present_patch_indicator": present_patch_indicator, "surviving_patch_indicator": surviving_patch_indicator, "proprietor_rows": proprietor_rows}


def enlarge_patches(sieve_pattern):
    return jnp.repeat(jnp.repeat(sieve_pattern, BLOCK, 0), BLOCK, 1)


def slot_numbers(proprietor_rows):
    per_holder_share = proprietor_rows.reshape(N_ROW, RB, N_COL, CB).transpose(0, 2, 1, 3).reshape(N_ROW, N_COL, RB * CB)
    same = per_holder_share[:, :, :, None] == per_holder_share[:, :, None, :]
    index = jnp.arange(RB * CB, dtype=jnp.int32)
    earlier = index[None, :] < index[:, None]
    counted = jnp.sum((same & earlier[None, None]).astype(jnp.int32), axis=3).astype(jnp.int32)
    return counted.reshape(N_ROW, N_COL, RB, CB).transpose(0, 2, 1, 3).reshape(TILES_ACROSS, TILES_ACROSS)


def reference(unsieved_electron_density, present_patch_indicator, surviving_patch_indicator, proprietor_rows):
    sieved_electron_density = unsieved_electron_density * enlarge_patches(present_patch_indicator).astype(jnp.bfloat16)
    density_times_itself = jnp.dot(sieved_electron_density, sieved_electron_density, preferred_element_type=jnp.float32)
    thinned_self_multiply = density_times_itself * enlarge_patches(surviving_patch_indicator).astype(jnp.float32)
    squared = thinned_self_multiply.astype(jnp.bfloat16)
    cubed = jnp.dot(squared, sieved_electron_density, preferred_element_type=jnp.float32)
    purified = (3.0 * thinned_self_multiply - 2.0 * cubed).astype(jnp.bfloat16)
    blocks = purified.reshape(TILES_ACROSS, BLOCK, TILES_ACROSS, BLOCK).transpose(0, 2, 1, 3).reshape(TILES_ACROSS * TILES_ACROSS, BLOCK * BLOCK)
    source_row = jnp.broadcast_to((jnp.arange(TILES_ACROSS, dtype=jnp.int32) // RB)[:, None], (TILES_ACROSS, TILES_ACROSS))
    column_group = jnp.broadcast_to((jnp.arange(TILES_ACROSS, dtype=jnp.int32) // CB)[None, :], (TILES_ACROSS, TILES_ACROSS))
    slot = slot_numbers(proprietor_rows)
    first_index = ((proprietor_rows * N_ROW + source_row) * SLOTS + slot).reshape(-1).astype(jnp.int32)
    second_index = column_group.reshape(-1).astype(jnp.int32)
    delivered = jnp.zeros((N_ROW * N_ROW * SLOTS, N_COL, BLOCK * BLOCK), jnp.bfloat16)
    return delivered.at[first_index, second_index].set(blocks)
```

```python
import functools

import jax
import jax.numpy as jnp
from jax import lax
from jax.experimental import pallas as pl
from jax.experimental.pallas import tpu as pltpu
from jax.sharding import PartitionSpec as P

MESH = pl.DeviceIdType.MESH
B = 128
ROWS = 512
COLS = 1024
NCH = 4
W = COLS // NCH
SUB = ROWS // W
HS = SUB // 2
BW = W // B
F32 = jnp.float32
BF16 = jnp.bfloat16


def coords():
    r = lax.axis_index("row")
    c = lax.axis_index("col")
    return (r // 2) % 4, (r // 8) * 2 + c % 2, c // 2, r % 2


def dev(x, y, z, core):
    x = (x + 8) % 4
    y = (y + 8) % 4
    z = (z + 8) % 4
    return ((y // 2) * 8 + x * 2 + core, z * 2 + y % 2)


def cols(at, width=W):
    return pl.ds(pl.multiple_of(at * W, W), width)


def step_kernel(
    u, present, surviving, out,
    own, right, left, fleft, fown, sums, ssend, srecv, csend, crecv, total,
    s1s, s1r, s2s, s2r, s3s, s3r, ds_, dr, loc, ls, lr, lrs, lrr, fs, fr, frs, frr, xs, xr, cs, cr,
):
    x, y, z, core = coords()
    yl = y % 2
    q = (x + y) % 2
    here = (x, y, z, core)
    bar = pltpu.get_barrier_semaphore()
    near = [
        dev(x + 1, y, z, core), dev(x - 1, y, z, core), dev(x, y + 1, z, core), dev(x, y - 1, z, core),
        dev(x, y + 2, z, core), dev(x, y, z + 1, core), dev(x, y, z - 1, core), dev(x, y, z, 1 - core),
    ]
    xp, xm, yp, ym, yy, zp, zm, other = near
    partner = dev(x, (y // 2) * 2 + 1 - yl, z, core)
    for d in near:
        pl.semaphore_signal(bar, inc=1, device_id=d, device_id_type=MESH)

    def rc(src, dst, ssem, rsem, to):
        return pltpu.make_async_remote_copy(
            src_ref=src, dst_ref=dst, send_sem=ssem, recv_sem=rsem, device_id=to, device_id_type=MESH
        )

    pending = []

    def go(copy):
        copy.start()
        pending.append(copy)

    def piece(j, xs_, ys_, h):
        xs_ = (xs_ + 8) % 4
        ys_ = (ys_ + 8) % 4
        slab = (ys_ // 2) * 2 + xs_ // 2
        k = core * (NCH // 2) + h * HS
        return right.at[j, pl.ds(k, HS), slab, :, cols(ys_ % 2)]

    def sieve(j):
        for i in range(4):
            for b in range(BW):
                keep = present[i, j * BW + b] != 0
                block = u[i * B:(i + 1) * B, j * W + b * B:j * W + (b + 1) * B]
                r0 = (i * B) % W
                kept = jnp.where(keep, block, jnp.zeros_like(block))
                own[0, j, (i * B) // W, r0:r0 + B, b * B:(b + 1) * B] = kept

    def st1(j):
        for h in range(2):
            part = pl.ds(h * HS, HS)
            go(rc(own.at[0, j, part], own.at[1, j, part], s1s.at[j, h], s1r.at[j, h], xm if h else xp))

    def st1_wait(j):
        for h in range(2):
            part = pl.ds(h * HS, HS)
            rc(own.at[0, j, part], own.at[1, j, part], s1s.at[j, h], s1r.at[j, h], xp).wait_recv()

    def shift(h):
        return 1 if h else -1

    def st2(j):
        st1_wait(j)
        locals_ = []
        for h in range(2):
            part = pl.ds(h * HS, HS)
            wrong = own.at[1 - q, j, part]
            fine = own.at[q, j, part]
            wx = x + (1 - q) * shift(h)
            fx = x + q * shift(h)
            go(rc(wrong, piece(j, wx, y, h), s2s.at[j, h, 0], s2r.at[j, h, 0], yp))
            go(rc(wrong, piece(j, wx, y, h), s2s.at[j, h, 1], s2r.at[j, h, 1], ym))
            go(rc(fine, piece(j, fx, y, h), s2s.at[j, h, 2], s2r.at[j, h, 2], yy))
            c = pltpu.make_async_copy(fine, piece(j, fx, y, h), loc.at[j, h])
            c.start()
            locals_.append(c)
        return locals_

    def st3(j, locals_):
        for d, kind in ((0, None), (-1, 0), (1, 1), (2, 2)):
            for h in range(2):
                at = piece(j, x + q * shift(h), y + d, h)
                if kind is None:
                    locals_[h].wait()
                else:
                    rc(at, at, s2s.at[j, h, kind], s2r.at[j, h, kind], yp).wait_recv()
                n = d % 4
                to = dev(x + shift(h) * (1 - 2 * q), y, z, core)
                go(rc(at, at, s3s.at[j, n, h], s3r.at[j, n, h], to))
                rc(at, at, ds_.at[j], dr.at[j], other).start()

    def share(j):
        for d in (0, -1, 1, 2):
            for h in range(2):
                at = piece(j, x + q * shift(h) + 2, y + d, h)
                rc(at, at, s3s.at[j, d % 4, h], s3r.at[j, d % 4, h], xp).wait_recv()
                rc(at, at, ds_.at[j], dr.at[j], other).start()

    def half(j, c):
        return right.at[j, pl.ds(c * (NCH // 2), NCH // 2)]

    def ring_send(src, buf, j, ssem, rsem):
        go(rc(src, buf.at[j, :, :, cols(z)], ssem.at[j, 0], rsem.at[j, 0], zp))
        go(rc(src, buf.at[j, :, :, cols(z)], ssem.at[j, 1], rsem.at[j, 1], zm))

    def ring_relay(buf, j, ssem, rsem, rss, rsr):
        for k, (frm, to) in enumerate(((-1, zp), (1, zm))):
            at = buf.at[j, :, :, cols((z + frm + 4) % 4)]
            rc(at, at, ssem.at[j, k], rsem.at[j, k], to).wait_recv()
            on = buf.at[j, pl.ds(k * HS, HS), :, cols((z + frm + 4) % 4)]
            go(rc(on, on, rss.at[j, k], rsr.at[j, k], to))

    def ring_wait(buf, j, rss, rsr):
        for k in range(2):
            at = buf.at[j, pl.ds(k * HS, HS), :, cols((z + 2) % 4)]
            rc(at, at, rss.at[j, k], rsr.at[j, k], zp).wait_recv()

    def square(j):
        rc(half(j, core), half(j, 1 - core), ds_.at[j], dr.at[j], other).wait_recv()

        @pl.loop(0, SUB)
        def _(m):
            acc = None
            for k in range(NCH):
                d = jnp.dot(left[k, m], right[j, k].reshape(4 * W, 2 * W), preferred_element_type=F32)
                acc = d if acc is None else acc + d
            sums[m] = acc

        @pl.loop(0, SUB)
        def _(m):
            ssend[j, m] = sums[m, :, cols(1 - yl)].astype(BF16)

        go(rc(ssend.at[j], srecv.at[j], xs.at[j], xr.at[j], partner))

    def sift(j):
        rc(ssend.at[j], srecv.at[j], xs.at[j], xr.at[j], partner).wait_recv()
        for i in range(4):
            m, r0 = (i * B) // W, (i * B) % W
            for b in range(BW):
                keep = surviving[i, j * BW + b].astype(F32)
                mine = pl.ds(pl.multiple_of(yl * W + b * B, B), B)
                theirs = pl.ds(pl.multiple_of((1 - yl) * W + b * B, B), B)
                rows, cb = slice(r0, r0 + B), slice(b * B, (b + 1) * B)
                f = (sums[m, rows, mine] + srecv[j, m, rows, cb].astype(F32)) * keep
                fb = f.astype(BF16)
                fown[j, m, rows, cb] = fb
                fleft[j, m, rows, pl.ds(pl.multiple_of(z * W + b * B, B), B)] = fb
                total[j, m, rows, mine] = f * -1.5
                total[j, m, rows, theirs] = jnp.zeros((B, B), F32)
        ring_send(fown.at[j], fleft, j, fs, fr)

    def cube(ks, j):
        if not ks:
            return

        @pl.loop(0, SUB)
        def _(m):
            acc = total[j, m]
            for k in ks:
                acc += jnp.dot(fleft[k, m], right[j, k].reshape(4 * W, 2 * W), preferred_element_type=F32)
            total[j, m] = acc

    def cube_send(j):
        @pl.loop(0, SUB)
        def _(m):
            csend[j, m] = total[j, m, :, cols(1 - yl)].astype(BF16)

        go(rc(csend.at[j], crecv.at[j], cs.at[j], cr.at[j], partner))

    def finish(j):
        rc(csend.at[j], crecv.at[j], cs.at[j], cr.at[j], partner).wait_recv()
        for i in range(4):
            m, r0 = (i * B) // W, (i * B) % W
            for b in range(BW):
                mine = pl.ds(pl.multiple_of(yl * W + b * B, B), B)
                rows, cb = slice(r0, r0 + B), slice(b * B, (b + 1) * B)
                v = (total[j, m, rows, mine] + crecv[j, m, rows, cb].astype(F32)) * -2.0
                out[i * 8 + j * BW + b] = v.astype(BF16)

    own_lefts = []
    sieve(0)
    pl.semaphore_wait(bar, 8)
    st1(0)
    for j in range(NCH):
        if j:
            sieve(j)
        if j == 1:
            st1(1)
        own_left = pltpu.make_async_copy(own.at[0, j], left.at[j, :, :, cols(z)], lrs.at[j, 2])
        own_left.start()
        own_lefts.append(own_left)
        ring_send(own.at[0, j], left, j, ls, lr)

    held = {}
    fdone = 0
    done = {j: 0 for j in range(NCH)}
    left_relays = {0: [0], 1: list(range(1, NCH - 1)), 2: [NCH - 1]}
    for t in range(NCH + 2):
        if t < NCH:
            held[t] = st2(t)
            if t + 2 < NCH:
                st1(t + 2)
        if 0 <= t - 1 < NCH:
            st3(t - 1, held[t - 1])
        for j in left_relays.get(t, []):
            ring_relay(left, j, ls, lr, lrs, lrr)
        s = t - 2
        if 0 <= s:
            share(s)
            if s == 0:
                for j in range(NCH):
                    ring_wait(left, j, lrs, lrr)
                    own_lefts[j].wait()
            square(s)
            if s >= 1:
                ring_relay(fleft, s - 1, fs, fr, frs, frr)
            if s >= 2:
                ring_wait(fleft, s - 2, frs, frr)
                fdone = s - 1
            for j in range(s):
                cube(list(range(done[j], fdone)), j)
                done[j] = fdone
            sift(s)
    last = NCH - 1
    if NCH >= 2:
        ring_wait(fleft, last - 1, frs, frr)
        for j in range(NCH):
            cube(list(range(done[j], last)), j)
    ring_relay(fleft, last, fs, fr, frs, frr)
    ring_wait(fleft, last, frs, frr)
    for j in range(NCH):
        cube([last], j)
        cube_send(j)
    for j in range(NCH):
        rc(half(j, core), half(j, 1 - core), ds_.at[j], dr.at[j], other).wait_send()
    for c in pending[:-NCH]:
        c.wait_send()
    for j in range(NCH):
        finish(j)
    for c in pending[-NCH:]:
        c.wait_send()


def deliver_kernel(p, index, valid, out, packed, ss, rs, loc):
    r = lax.axis_index("row")
    c = lax.axis_index("col")
    n = 16
    bar = pltpu.get_barrier_semaphore()
    for d in range(1, n):
        pl.semaphore_signal(bar, inc=1, device_id=((r + d) % n, c), device_id_type=MESH)

    @pl.loop(0, 64)
    def _(s):
        block = p[index[s]]
        packed[s] = jnp.where(valid[s] != 0, block, jnp.zeros_like(block))

    pl.semaphore_wait(bar, n - 1)
    mine = pltpu.make_async_copy(packed.at[pl.ds(r * 4, 4)], out.at[pl.ds(r * 4, 4)], loc)
    mine.start()
    copies = []
    for d in range(1, n):
        to = (r + d) % n
        copy = pltpu.make_async_remote_copy(
            src_ref=packed.at[pl.ds(to * 4, 4)], dst_ref=out.at[pl.ds(r * 4, 4)],
            send_sem=ss.at[d], recv_sem=rs.at[d], device_id=(to, c), device_id_type=MESH,
        )
        copy.start()
        copies.append(copy)
    mine.wait()
    for copy in copies:
        copy.wait()


def slots(owners):
    flat = owners.reshape(-1)
    at = jnp.arange(32, dtype=jnp.int32)
    same = flat[:, None] == flat[None, :]
    slot = jnp.sum((same & (at[None, :] < at[:, None])).astype(jnp.int32), axis=1)
    target = flat * 4 + slot
    hit = target[None, :] == jnp.arange(64, dtype=jnp.int32)[:, None]
    return jnp.sum(jnp.where(hit, at[None, :], 0), axis=1), jnp.sum(hit.astype(jnp.int32), axis=1)


def per_device(u, present, surviving, owners):
    vm = pl.BlockSpec(memory_space=pltpu.VMEM)
    sm = pl.BlockSpec(memory_space=pltpu.SMEM)
    dma = pltpu.SemaphoreType.DMA
    vmem = pltpu.VMEM
    index, valid = slots(owners)
    purified = pl.pallas_call(
        step_kernel,
        out_shape=jax.ShapeDtypeStruct((32, B, B), BF16),
        in_specs=[vm, sm, sm],
        out_specs=vm,
        scratch_shapes=[
            vmem((2, NCH, SUB, W, W), BF16),
            vmem((NCH, NCH, 4, W, 2 * W), BF16),
            vmem((NCH, SUB, W, 4 * W), BF16),
            vmem((NCH, SUB, W, 4 * W), BF16),
            vmem((NCH, SUB, W, W), BF16),
            vmem((SUB, W, 2 * W), F32),
            vmem((NCH, SUB, W, W), BF16),
            vmem((NCH, SUB, W, W), BF16),
            vmem((NCH, SUB, W, W), BF16),
            vmem((NCH, SUB, W, W), BF16),
            vmem((NCH, SUB, W, 2 * W), F32),
            dma((NCH, 2)), dma((NCH, 2)),
            dma((NCH, 2, 3)), dma((NCH, 2, 3)),
            dma((NCH, 4, 2)), dma((NCH, 4, 2)),
            dma((NCH,)), dma((NCH,)), dma((NCH, 2)),
            dma((NCH, 2)), dma((NCH, 2)), dma((NCH, 3)), dma((NCH, 2)),
            dma((NCH, 2)), dma((NCH, 2)), dma((NCH, 2)), dma((NCH, 2)),
            dma((NCH,)), dma((NCH,)), dma((NCH,)), dma((NCH,)),
        ],
        compiler_params=pltpu.CompilerParams(
            collective_id=0, has_side_effects=True, vmem_limit_bytes=56 * 2**20
        ),
        cost_estimate=pl.CostEstimate(flops=17179869184, bytes_accessed=2 * 2**20, transcendentals=0),
        name="step",
    )(u, present, surviving)
    arrived = pl.pallas_call(
        deliver_kernel,
        out_shape=jax.ShapeDtypeStruct((64, B, B), BF16),
        in_specs=[vm, sm, sm],
        out_specs=vm,
        scratch_shapes=[vmem((64, B, B), BF16), dma((16,)), dma((16,)), dma],
        compiler_params=pltpu.CompilerParams(
            collective_id=1, has_side_effects=True, vmem_limit_bytes=24 * 2**20
        ),
        name="deliver",
    )(purified, index, valid)
    return arrived.reshape(64, 1, B * B)


def solution(mesh):
    placed = (P("row", "col"), P("row", "col"), P("row", "col"), P("row", "col"))
    return jax.shard_map(
        per_device, mesh=mesh, in_specs=placed, out_specs=P("row", "col", None), check_vma=False
    )
```

```python
import jax
import jax.numpy as jnp
from jax import lax
from jax.experimental import pallas as pl
from jax.experimental.pallas import tpu as pltpu
from jax.sharding import PartitionSpec as P

MESH = pl.DeviceIdType.MESH
B = 128
ROWS = 512
COLS = 1024
NCH = 4
W = COLS // NCH
SUB = ROWS // W
HS = SUB // 2
UNITS = ((0, 0, 256), (1, 0, 256), (2, 0, 256), (3, 0, 128), (3, 128, 128))
NU = len(UNITS)
BW = W // B
ACROSS = ((2, 0), (2, 1), (1, 0), (3, 1), (3, 0), (1, 1), (0, 1), (0, 0))
F32 = jnp.float32
BF16 = jnp.bfloat16


def coords():
    r = lax.axis_index("row")
    c = lax.axis_index("col")
    return (r // 2) % 4, (r // 8) * 2 + c % 2, c // 2, r % 2


def dev(x, y, z, core):
    x = (x + 8) % 4
    y = (y + 8) % 4
    z = (z + 8) % 4
    return ((y // 2) * 8 + x * 2 + core, z * 2 + y % 2)


def cube_up(chunks, upto, met, cube):
    groups = {}
    for j in chunks:
        groups.setdefault(met.get(j, 0), []).append(j)
        met[j] = upto
    for first, js in groups.items():
        cube(list(range(first, upto)), js[0], js[-1] + 1)


def cols(at, width=W):
    return pl.ds(pl.multiple_of(at * W, W), width)


def step_kernel(
    u, present, surviving, index, valid, out,
    own, right, left, fleft, fown, sums, ssend, srecv, csend, crecv, total, blocks, packed, landed,
    s1s, s1r, s2s, s2r, s3s, s3r, ds_, dr, loc, ls, lr, lrs, lrr, fs, fr, frs, frr, xs, xr, cs, cr, as_, ar,
):
    x, y, z, core = coords()
    yl = y % 2
    q = (x + y) % 2
    bar = pltpu.get_barrier_semaphore()
    xp, xm = dev(x + 1, y, z, core), dev(x - 1, y, z, core)
    yp, ym, yy = dev(x, y + 1, z, core), dev(x, y - 1, z, core), dev(x, y + 2, z, core)
    zp, zm = dev(x, y, z + 1, core), dev(x, y, z - 1, core)
    other = dev(x, y, z, 1 - core)
    partner = dev(x, (y // 2) * 2 + 1 - yl, z, core)
    near = [yp, ym, yy, zp, zm]
    near += [dev(x + dx, y, z, (core + dc) % 2) for dx, dc in ACROSS if (dx, dc) != (0, 0)]
    for d in near:
        pl.semaphore_signal(bar, inc=1, device_id=d, device_id_type=MESH)

    def rc(src, dst, ssem, rsem, to):
        return pltpu.make_async_remote_copy(
            src_ref=src, dst_ref=dst, send_sem=ssem, recv_sem=rsem, device_id=to, device_id_type=MESH
        )

    pending = []

    def go(copy):
        copy.start()
        pending.append(copy)

    def piece(n, xs_, ys_, h):
        xs_ = (xs_ + 8) % 4
        ys_ = (ys_ + 8) % 4
        k = core * (NCH // 2) + h * HS
        j, c, w = UNITS[n]
        return right.at[j, pl.ds(k, HS), ys_ // 2, xs_ // 2, :, pl.ds(pl.multiple_of((ys_ % 2) * W + c, B), w)]

    def sieve(j):
        for i in range(4):
            for b in range(BW):
                keep = present[i, j * BW + b] != 0
                block = u[i * B:(i + 1) * B, j * W + b * B:j * W + (b + 1) * B]
                r0 = (i * B) % W
                kept = jnp.where(keep, block, jnp.zeros_like(block))
                own[0, j, (i * B) // W, r0:r0 + B, b * B:(b + 1) * B] = kept

    def part(h):
        return pl.ds(h * HS, HS)

    def shift(h):
        return 1 if h else -1

    def mine(g, n, h):
        j, c, w = UNITS[n]
        return own.at[g, j, part(h), :, pl.ds(c, w)]

    def st1(n):
        for h in range(2):
            go(rc(mine(0, n, h), mine(1, n, h), s1s.at[n, h], s1r.at[n, h], xm if h else xp))

    def along_x(j, h, d, src):
        at = piece(j, x + q * shift(h), y + d, h)
        to = dev(x + shift(h) * (1 - 2 * q), y, z, core)
        go(rc(at if src is None else src, at, s3s.at[j, d % 4, h], s3r.at[j, d % 4, h], to))

    def st1_wait(n):
        for h in range(2):
            rc(mine(0, n, h), mine(1, n, h), s1s.at[n, h], s1r.at[n, h], xp).wait_recv()

    def st2(n):
        for h in range(2):
            wrong = mine(1 - q, n, h)
            fine = mine(q, n, h)
            wx = x + (1 - q) * shift(h)
            fx = x + q * shift(h)
            go(rc(wrong, piece(n, wx, y, h), s2s.at[n, h, 0], s2r.at[n, h, 0], yp))
            go(rc(wrong, piece(n, wx, y, h), s2s.at[n, h, 1], s2r.at[n, h, 1], ym))
            go(rc(fine, piece(n, fx, y, h), s2s.at[n, h, 2], s2r.at[n, h, 2], yy))

    def st2_here(n):
        for h in range(2):
            fine = mine(q, n, h)
            along_x(n, h, 0, fine)
            pltpu.make_async_copy(fine, piece(n, x + q * shift(h), y, h), loc.at[n, h]).start()

    def hand_over(n, xs_, h):
        j, c, w = UNITS[n]
        k = core * (NCH // 2) + h * HS
        for c0, wide in ((0, 2 * W),) if w == W else ((c, w), (W + c, w)):
            at = right.at[j, pl.ds(k, HS), :, ((xs_ + 8) % 4) // 2, :, pl.ds(c0, wide)]
            rc(at, at, ds_.at[n], dr.at[n], other).start()

    def st3(j, kinds):
        for kind in kinds:
            for h in range(2):
                d = (-1, 1, 2)[kind]
                at = piece(j, x + q * shift(h), y + d, h)
                rc(at, at, s2s.at[j, h, kind], s2r.at[j, h, kind], yp).wait_recv()
                along_x(j, h, d, None)

    def share_first(j):
        for h in range(2):
            at = mine(q, j, h)
            pltpu.make_async_copy(at, piece(j, x + q * shift(h), y, h), loc.at[j, h]).wait()
            hand_over(j, x + q * shift(h), h)

    def share(j):
        for h in range(2):
            for d in (0, -1, 1, 2):
                at = piece(j, x + q * shift(h) + 2, y + d, h)
                rc(at, at, s3s.at[j, d % 4, h], s3r.at[j, d % 4, h], xp).wait_recv()
            hand_over(j, x + q * shift(h) + 2, h)

    def half(n, core_):
        j, c, w = UNITS[n]
        k = pl.ds(core_ * (NCH // 2), NCH // 2)
        return right.at[j, k, :, :, :, pl.ds(0, 2 * w)]

    def l_send(j, k):
        return rc(own.at[0, j], left.at[j, :, :, cols(z)], ls.at[j, k], lr.at[j, k], (zp, zm)[k])

    def l_relay(j, k):
        on = left.at[j, part(k), :, cols((z + (3, 1)[k]) % 4)]
        return rc(on, on, lrs.at[j, k], lrr.at[j, k], (zp, zm)[k])

    def f_send(n, m, k):
        j, c, w = UNITS[n]
        at = fleft.at[j, m, :, pl.ds(pl.multiple_of(z * W + c, B), w)]
        return rc(fown.at[j, m, :, pl.ds(c, w)], at, fs.at[n, m, k], fr.at[n, m, k], (zp, zm)[k])

    def f_relay(n, m, k):
        j, c, w = UNITS[n]
        lane = pl.multiple_of(((z + (3, 1)[k]) % 4) * W + c, B)
        on = fleft.at[j, m, pl.ds(k * (W // 2), W // 2), pl.ds(lane, w)]
        return rc(on, on, frs.at[n, m, k], frr.at[n, m, k], (zp, zm)[k])

    def s_send(n, m):
        j, c, w = UNITS[n]
        at = pl.ds(c, w)
        return rc(ssend.at[j, m, :, at], srecv.at[j, m, :, at], xs.at[n, m], xr.at[n, m], partner)

    def c_send(j, m):
        return rc(csend.at[j, m], crecv.at[j, m], cs.at[j, m], cr.at[j, m], partner)

    def own_left(j):
        return pltpu.make_async_copy(own.at[0, j], left.at[j, :, :, cols(z)], ls.at[j, 2])

    def square(n):
        j, c, w = UNITS[n]
        rc(half(n, core), half(n, 1 - core), ds_.at[n], dr.at[n], other).wait_recv()

        @pl.loop(0, SUB)
        def _(m):
            acc = None
            for k in range(NCH):
                if w == W:
                    r = right[j, k].reshape(4 * W, 2 * W)
                else:
                    r = [right[j, k, :, :, :, c0:c0 + w].reshape(4 * W, w) for c0 in (c, W + c)]
                    r = jnp.concatenate(r, axis=1)
                d = jnp.dot(left[k, m], r, preferred_element_type=F32)
                acc = d if acc is None else acc + d
            sums[m, :, 0:2 * w] = acc
            ssend[j, m, :, c:c + w] = sums[m, :, pl.ds(pl.multiple_of((1 - yl) * w, B), w)].astype(BF16)
            s_send(n, m).start()

    def sift(n):
        j, c, w = UNITS[n]

        @pl.loop(0, SUB)
        def _(m):
            s_send(n, m).wait_recv()
            for i in range(W // B):
                rows = slice(i * B, (i + 1) * B)
                for b in range(c // B, (c + w) // B):
                    keep = surviving[m * (W // B) + i, j * BW + b].astype(F32)
                    at = pl.ds(pl.multiple_of(yl * w + b * B - c, B), B)
                    mine_ = pl.ds(pl.multiple_of(yl * W + b * B, B), B)
                    cb = slice(b * B, (b + 1) * B)
                    f = (sums[m, rows, at] + srecv[j, m, rows, cb].astype(F32)) * keep
                    fb = f.astype(BF16)
                    fown[j, m, rows, cb] = fb
                    fleft[j, m, rows, pl.ds(pl.multiple_of(z * W + b * B, B), B)] = fb
                    total[j, m, rows, mine_] = total[j, m, rows, mine_] + f * -1.5
            for k in range(2):
                f_send(n, m, k).start()

    def sift_relay(j):
        @pl.loop(0, SUB)
        def _(m):
            for k in range(2):
                f_send(j, m, k).wait_recv()
                f_relay(j, m, k).start()

    def sift_wait(j):
        @pl.loop(0, SUB)
        def _(m):
            for k in range(2):
                f_relay(j, m, k).wait_recv()

    def cubed(n, j, m):
        k, c, w = UNITS[n]
        if w == W:
            return jnp.dot(fleft[k, m], right[j, k].reshape(4 * W, 2 * W), preferred_element_type=F32)
        f = jnp.concatenate([fleft[k, m, :, i * W + c:i * W + c + w] for i in range(4)], axis=1)
        r = right[j, k, :, :, c:c + w, :].reshape(4 * w, 2 * W)
        return jnp.dot(f, r, preferred_element_type=F32)

    def cube(ns, j0, j1):
        if not len(ns) or j0 >= j1:
            return

        @pl.loop(j0, j1)
        def _(j):
            @pl.loop(0, SUB)
            def _(m):
                acc = total[j, m]
                for n in ns:
                    acc += cubed(n, j, m)
                total[j, m] = acc

    last = NU - 1
    sieve(0)
    pl.semaphore_wait(bar, len(near))
    st1(0)
    for j in range(NCH):
        if j:
            sieve(j)
        own_left(j).start()
        for k in range(2):
            l_send(j, k).start()
    st1(1)

    met = {}
    for t in range(NU + 2):
        s = t - 2
        if 1 <= t <= NU:
            st3(t - 1, (0,))
        if t == 0:
            st1_wait(0)
            st2(0)
            st2_here(0)
            for n in range(2, NU):
                st1(n)
            st1_wait(1)
            st2_here(1)
            total[...] = jnp.zeros_like(total)
        elif t < NU:
            st2(t)
            if t + 1 < NU:
                st1_wait(t + 1)
                st2_here(t + 1)
        if 1 <= t <= NU:
            st3(t - 1, (1, 2))
            share_first(t - 1)
        if s >= 1:
            sift(s - 1)
        if t == 1:
            for j in range(NCH):
                for k in range(2):
                    l_send(j, k).wait_recv()
                    l_relay(j, k).start()
        if s < 0:
            continue
        share(s)
        if s == 0:
            for j in range(NCH):
                own_left(j).wait()
                for k in range(2):
                    l_relay(j, k).wait_recv()
        square(s)
        if s >= 1:
            sift_relay(s - 1)
        if s >= 2:
            sift_wait(s - 2)
            ready = [j for j in range(NCH) if all(n <= s for n in range(NU) if UNITS[n][0] == j)]
            cube_up(ready, s - 1, met, cube)
    sift(last)
    sift_wait(last - 1)
    cube_up(list(range(NCH)), last, met, cube)
    sift_relay(last)

    @pl.loop(0, SUB)
    def _(m):
        for k in range(2):
            f_relay(last, m, k).wait_recv()

        @pl.loop(0, NCH)
        def _(j):
            total[j, m] = total[j, m] + cubed(last, j, m)
            csend[j, m] = total[j, m, :, cols(1 - yl)].astype(BF16)
            c_send(j, m).start()

    for copy in pending:
        copy.wait_send()
    for n in range(NU):
        rc(half(n, core), half(n, 1 - core), ds_.at[n], dr.at[n], other).wait_send()
    for j in range(NCH):
        for k in range(2):
            l_send(j, k).wait_send()
            l_relay(j, k).wait_send()
    for n in range(NU):
        for m in range(SUB):
            s_send(n, m).wait_send()
            for k in range(2):
                f_send(n, m, k).wait_send()
                f_relay(n, m, k).wait_send()

    @pl.loop(0, SUB)
    def _(m):
        @pl.loop(0, NCH)
        def _(j):
            c_send(j, m).wait_recv()
            for i in range(W // B):
                for b in range(BW):
                    mine_ = pl.ds(pl.multiple_of(yl * W + b * B, B), B)
                    rows, cb = slice(i * B, (i + 1) * B), slice(b * B, (b + 1) * B)
                    v = (total[j, m, rows, mine_] + crecv[j, m, rows, cb].astype(F32)) * -2.0
                    blocks[(m * (W // B) + i) * 8 + j * BW + b] = v.astype(BF16)

    r = lax.axis_index("row")

    def slot(s):
        block = blocks[index[s]]
        return jnp.where(valid[s] != 0, block, jnp.zeros_like(block))

    there = dev(x, y + 2, z, core)
    copies = []
    for n, (dx, dc) in enumerate(ACROSS):
        to = dev(x + dx, y + 2, z, (core + dc) % 2)
        at = to[0] * 4
        for k in range(4):
            packed[at + k] = slot(at + k)
        copies.append(rc(packed.at[pl.ds(at, 4)], landed.at[n], as_.at[n], ar.at[n], there))
        copies[-1].start()
    for n, (dx, dc) in enumerate(ACROSS):
        if (dx, dc) == (0, 0):
            continue
        to = dev(x + dx, y, z, (core + dc) % 2)
        at = to[0] * 4
        for k in range(4):
            packed[at + k] = slot(at + k)
        copies.append(rc(packed.at[pl.ds(at, 4)], out.at[pl.ds(r * 4, 4)], as_.at[8 + n], ar.at[8 + n], to))
        copies[-1].start()
    for k in range(4):
        out[r * 4 + k] = slot(r * 4 + k)
    for n, (dx, dc) in enumerate(ACROSS):
        to = dev(x + dx, y, z, (core + dc) % 2)
        copies[n].wait_recv()
        at = out.at[pl.ds(there[0] * 4, 4)]
        if (dx, dc) == (0, 0):
            stay = pltpu.make_async_copy(landed.at[n], at, as_.at[16 + n])
            stay.start()
        else:
            copies.append(rc(landed.at[n], at, as_.at[16 + n], ar.at[16 + n], to))
            copies[-1].start()

    @pl.loop(0, NCH)
    def _(j):
        @pl.loop(0, SUB)
        def _(m):
            c_send(j, m).wait_send()

    stay.wait()
    for n, copy in enumerate(copies):
        copy.wait_send()
        if n >= 8:
            copy.wait_recv()


def slots(owners):
    flat = owners.reshape(-1)
    at = jnp.arange(32, dtype=jnp.int32)
    same = flat[:, None] == flat[None, :]
    slot = jnp.sum((same & (at[None, :] < at[:, None])).astype(jnp.int32), axis=1)
    target = flat * 4 + slot
    hit = target[None, :] == jnp.arange(64, dtype=jnp.int32)[:, None]
    return jnp.sum(jnp.where(hit, at[None, :], 0), axis=1), jnp.sum(hit.astype(jnp.int32), axis=1)


def per_device(u, present, surviving, owners):
    vm = pl.BlockSpec(memory_space=pltpu.VMEM)
    sm = pl.BlockSpec(memory_space=pltpu.SMEM)
    dma = pltpu.SemaphoreType.DMA
    vmem = pltpu.VMEM
    index, valid = slots(owners)
    arrived = pl.pallas_call(
        step_kernel,
        out_shape=jax.ShapeDtypeStruct((64, B, B), BF16),
        in_specs=[vm, sm, sm, sm, sm],
        out_specs=vm,
        scratch_shapes=[
            vmem((2, NCH, SUB, W, W), BF16),
            vmem((NCH, NCH, 2, 2, W, 2 * W), BF16),
            vmem((NCH, SUB, W, 4 * W), BF16),
            vmem((NCH, SUB, W, 4 * W), BF16),
            vmem((NCH, SUB, W, W), BF16),
            vmem((SUB, W, 2 * W), F32),
            vmem((NCH, SUB, W, W), BF16),
            vmem((NCH, SUB, W, W), BF16),
            vmem((NCH, SUB, W, W), BF16),
            vmem((NCH, SUB, W, W), BF16),
            vmem((NCH, SUB, W, 2 * W), F32),
            vmem((32, B, B), BF16),
            vmem((64, B, B), BF16),
            vmem((8, 4, B, B), BF16),
            dma((NU, 2)), dma((NU, 2)),
            dma((NU, 2, 3)), dma((NU, 2, 3)),
            dma((NU, 4, 2)), dma((NU, 4, 2)),
            dma((NU,)), dma((NU,)), dma((NU, 2)),
            dma((NCH, 3)), dma((NCH, 2)), dma((NCH, 2)), dma((NCH, 2)),
            dma((NU, SUB, 2)), dma((NU, SUB, 2)), dma((NU, SUB, 2)), dma((NU, SUB, 2)),
            dma((NU, SUB)), dma((NU, SUB)), dma((NCH, SUB)), dma((NCH, SUB)),
            dma((24,)), dma((24,)),
        ],
        compiler_params=pltpu.CompilerParams(
            collective_id=0, has_side_effects=True, vmem_limit_bytes=46 * 2**20
        ),
        cost_estimate=pl.CostEstimate(flops=17179869184, bytes_accessed=2 * 2**20, transcendentals=0),
        name="step",
    )(u, present, surviving, index, valid)
    return arrived.reshape(64, 1, B * B)


def solution(mesh):
    placed = (P("row", "col"), P("row", "col"), P("row", "col"), P("row", "col"))
    return jax.shard_map(
        per_device, mesh=mesh, in_specs=placed, out_specs=P("row", "col", None), check_vma=False
    )
```

```python
import jax
import jax.numpy as jnp
from jax import lax
from jax.experimental import pallas as pl
from jax.experimental.pallas import tpu as pltpu
from jax.sharding import PartitionSpec as P

MESH = pl.DeviceIdType.MESH
B = 128
ROWS = 512
COLS = 1024
NCH = 4
W = COLS // NCH
SUB = ROWS // W
HS = SUB // 2
UNITS = ((0, 0, 256), (1, 0, 256), (2, 0, 256), (3, 0, 128), (3, 128, 128))
NU = len(UNITS)
FLIGHT = 3
EARLY = 1
BW = W // B
ACROSS = ((2, 0), (2, 1), (1, 0), (3, 1), (3, 0), (1, 1), (0, 1), (0, 0))
F32 = jnp.float32
BF16 = jnp.bfloat16


def coords():
    r = lax.axis_index("row")
    c = lax.axis_index("col")
    return (r // 2) % 4, (r // 8) * 2 + c % 2, c // 2, r % 2


def dev(x, y, z, core):
    x = (x + 8) % 4
    y = (y + 8) % 4
    z = (z + 8) % 4
    return ((y // 2) * 8 + x * 2 + core, z * 2 + y % 2)


def cube_up(chunks, upto, met, cube):
    groups = {}
    for j in chunks:
        groups.setdefault(met.get(j, 0), []).append(j)
        met[j] = upto
    for first, js in groups.items():
        cube(list(range(first, upto)), js[0], js[-1] + 1)


def cols(at, width=W):
    return pl.ds(pl.multiple_of(at * W, W), width)


def step_kernel(
    u, present, surviving, owned, out,
    own, right, left, fleft, fown, sums, ssend, srecv, csend, crecv, total, blocks, packed, landed, index, valid,
    s1s, s1r, s2s, s2r, s3s, s3r, ds_, dr, loc, ls, lr, lrs, lrr, fs, fr, frs, frr, xs, xr, cs, cr, as_, ar,
):
    x, y, z, core = coords()
    yl = y % 2
    q = (x + y) % 2
    bar = pltpu.get_barrier_semaphore()
    xp, xm = dev(x + 1, y, z, core), dev(x - 1, y, z, core)
    yp, ym, yy = dev(x, y + 1, z, core), dev(x, y - 1, z, core), dev(x, y + 2, z, core)
    zp, zm = dev(x, y, z + 1, core), dev(x, y, z - 1, core)
    other = dev(x, y, z, 1 - core)
    partner = dev(x, (y // 2) * 2 + 1 - yl, z, core)
    near = [yp, ym, yy, zp, zm]
    near += [dev(x + dx, y, z, (core + dc) % 2) for dx, dc in ACROSS if (dx, dc) != (0, 0)]
    for d in near:
        pl.semaphore_signal(bar, inc=1, device_id=d, device_id_type=MESH)

    def rc(src, dst, ssem, rsem, to):
        return pltpu.make_async_remote_copy(
            src_ref=src, dst_ref=dst, send_sem=ssem, recv_sem=rsem, device_id=to, device_id_type=MESH
        )

    pending = []

    def go(copy):
        copy.start()
        pending.append(copy)

    def piece(n, xs_, ys_, h):
        xs_ = (xs_ + 8) % 4
        ys_ = (ys_ + 8) % 4
        k = core * (NCH // 2) + h * HS
        j, c, w = UNITS[n]
        return right.at[j, pl.ds(k, HS), ys_ // 2, xs_ // 2, :, pl.ds(pl.multiple_of((ys_ % 2) * W + c, B), w)]

    def number_slots():
        at = []
        for b in range(32):
            o = owned[b // 8, b % 8]
            rank = jnp.int32(0)
            for e in range(b):
                rank += (owned[e // 8, e % 8] == o).astype(jnp.int32)
            at.append(o * 4 + rank)

        @pl.loop(0, 64)
        def _(n):
            which, found = jnp.int32(0), jnp.int32(0)
            for b in range(32):
                hit = at[b] == n
                which = jnp.where(hit, b, which)
                found = jnp.where(hit, 1, found)
            index[n] = which
            valid[n] = found

    def sieve(j):
        for i in range(4):
            for b in range(BW):
                keep = present[i, j * BW + b] != 0
                block = u[i * B:(i + 1) * B, j * W + b * B:j * W + (b + 1) * B]
                r0 = (i * B) % W
                kept = jnp.where(keep, block, jnp.zeros_like(block))
                own[0, j, (i * B) // W, r0:r0 + B, b * B:(b + 1) * B] = kept

    def part(h):
        return pl.ds(h * HS, HS)

    def shift(h):
        return 1 if h else -1

    def mine(g, n, h):
        j, c, w = UNITS[n]
        return own.at[g, j, part(h), :, pl.ds(c, w)]

    def st1(n):
        for h in range(2):
            go(rc(mine(0, n, h), mine(1, n, h), s1s.at[n, h], s1r.at[n, h], xm if h else xp))

    def along_x(j, h, d, src):
        at = piece(j, x + q * shift(h), y + d, h)
        to = dev(x + shift(h) * (1 - 2 * q), y, z, core)
        go(rc(at if src is None else src, at, s3s.at[j, d % 4, h], s3r.at[j, d % 4, h], to))

    def st1_wait(n):
        for h in range(2):
            rc(mine(0, n, h), mine(1, n, h), s1s.at[n, h], s1r.at[n, h], xp).wait_recv()

    def st2(n):
        for h in range(2):
            wrong = mine(1 - q, n, h)
            fine = mine(q, n, h)
            wx = x + (1 - q) * shift(h)
            fx = x + q * shift(h)
            go(rc(wrong, piece(n, wx, y, h), s2s.at[n, h, 0], s2r.at[n, h, 0], yp))
            go(rc(wrong, piece(n, wx, y, h), s2s.at[n, h, 1], s2r.at[n, h, 1], ym))
            go(rc(fine, piece(n, fx, y, h), s2s.at[n, h, 2], s2r.at[n, h, 2], yy))

    def st2_here(n):
        for h in range(2):
            fine = mine(q, n, h)
            along_x(n, h, 0, fine)
            pltpu.make_async_copy(fine, piece(n, x + q * shift(h), y, h), loc.at[n, h]).start()

    def hand_over(n, xs_, h):
        j, c, w = UNITS[n]
        k = core * (NCH // 2) + h * HS
        for c0, wide in ((0, 2 * W),) if w == W else ((c, w), (W + c, w)):
            at = right.at[j, pl.ds(k, HS), :, ((xs_ + 8) % 4) // 2, :, pl.ds(c0, wide)]
            rc(at, at, ds_.at[n], dr.at[n], other).start()

    def st3(j, kinds):
        for kind in kinds:
            for h in range(2):
                d = (-1, 1, 2)[kind]
                at = piece(j, x + q * shift(h), y + d, h)
                rc(at, at, s2s.at[j, h, kind], s2r.at[j, h, kind], yp).wait_recv()
                along_x(j, h, d, None)

    def share_first(j):
        for h in range(2):
            at = mine(q, j, h)
            pltpu.make_async_copy(at, piece(j, x + q * shift(h), y, h), loc.at[j, h]).wait()
            hand_over(j, x + q * shift(h), h)

    def share(j):
        for h in range(2):
            for d in (0, -1, 1, 2):
                at = piece(j, x + q * shift(h) + 2, y + d, h)
                rc(at, at, s3s.at[j, d % 4, h], s3r.at[j, d % 4, h], xp).wait_recv()
            hand_over(j, x + q * shift(h) + 2, h)

    def half(n, core_):
        j, c, w = UNITS[n]
        k = pl.ds(core_ * (NCH // 2), NCH // 2)
        return right.at[j, k, :, :, :, pl.ds(0, 2 * w)]

    def l_send(m, k):
        at = left.at[:, m, :, cols(z)]
        return rc(own.at[0, :, m], at, ls.at[m, k], lr.at[m, k], (zp, zm)[k])

    def l_relay(m, k):
        on = left.at[:, m, pl.ds(k * (W // 2), W // 2), cols((z + (3, 1)[k]) % 4)]
        return rc(on, on, lrs.at[m, k], lrr.at[m, k], (zp, zm)[k])

    def f_send(n, m, k):
        j, c, w = UNITS[n]
        at = fleft.at[j, m, :, pl.ds(pl.multiple_of(z * W + c, B), w)]
        return rc(fown.at[j, m, :, pl.ds(c, w)], at, fs.at[n, m, k], fr.at[n, m, k], (zp, zm)[k])

    def f_relay(n, m, k):
        j, c, w = UNITS[n]
        lane = pl.multiple_of(((z + (3, 1)[k]) % 4) * W + c, B)
        on = fleft.at[j, m, pl.ds(k * (W // 2), W // 2), pl.ds(lane, w)]
        return rc(on, on, frs.at[n, m, k], frr.at[n, m, k], (zp, zm)[k])

    def s_send(n, m):
        j, c, w = UNITS[n]
        at = pl.ds(c, w)
        return rc(ssend.at[j, m, :, at], srecv.at[j, m, :, at], xs.at[n, m], xr.at[n, m], partner)

    def c_send(j, m):
        return rc(csend.at[j, m], crecv.at[j, m], cs.at[j, m], cr.at[j, m], partner)

    def own_left(j):
        return pltpu.make_async_copy(own.at[0, j], left.at[j, :, :, cols(z)], ls.at[j, 2])

    def square(n):
        j, c, w = UNITS[n]
        if n == 0:
            for i in range(NCH):
                own_left(i).wait()
        rc(half(n, core), half(n, 1 - core), ds_.at[n], dr.at[n], other).wait_recv()

        def rows(m):
            acc = None
            for k in range(NCH):
                if w == W:
                    r = right[j, k].reshape(4 * W, 2 * W)
                else:
                    r = [right[j, k, :, :, :, c0:c0 + w].reshape(4 * W, w) for c0 in (c, W + c)]
                    r = jnp.concatenate(r, axis=1)
                d = jnp.dot(left[k, m], r, preferred_element_type=F32)
                acc = d if acc is None else acc + d
            sums[m, :, 0:2 * w] = acc
            ssend[j, m, :, c:c + w] = sums[m, :, pl.ds(pl.multiple_of((1 - yl) * w, B), w)].astype(BF16)
            s_send(n, m).start()

        if n:
            pl.loop(0, SUB)(rows)
        else:
            for m in range(SUB):
                for k in range(2):
                    l_relay(m, k).wait_recv()
                rows(m)

    def sift(n, m0=0, m1=SUB):
        j, c, w = UNITS[n]

        @pl.loop(m0, m1)
        def _(m):
            s_send(n, m).wait_recv()
            for i in range(W // B):
                rows = slice(i * B, (i + 1) * B)
                for b in range(c // B, (c + w) // B):
                    keep = surviving[m * (W // B) + i, j * BW + b].astype(F32)
                    at = pl.ds(pl.multiple_of(yl * w + b * B - c, B), B)
                    mine_ = pl.ds(pl.multiple_of(yl * W + b * B, B), B)
                    cb = slice(b * B, (b + 1) * B)
                    f = (sums[m, rows, at] + srecv[j, m, rows, cb].astype(F32)) * keep
                    fb = f.astype(BF16)
                    fown[j, m, rows, cb] = fb
                    fleft[j, m, rows, pl.ds(pl.multiple_of(z * W + b * B, B), B)] = fb
                    total[j, m, rows, mine_] = total[j, m, rows, mine_] + f * -1.5
            for k in range(2):
                f_send(n, m, k).start()

    def sift_relay(j):
        @pl.loop(0, SUB)
        def _(m):
            for k in range(2):
                f_send(j, m, k).wait_recv()
                f_relay(j, m, k).start()

    def sift_wait(j):
        @pl.loop(0, SUB)
        def _(m):
            for k in range(2):
                f_relay(j, m, k).wait_recv()

    def cubed(n, j, m):
        k, c, w = UNITS[n]
        if w == W:
            return jnp.dot(fleft[k, m], right[j, k].reshape(4 * W, 2 * W), preferred_element_type=F32)
        f = jnp.concatenate([fleft[k, m, :, i * W + c:i * W + c + w] for i in range(4)], axis=1)
        r = right[j, k, :, :, c:c + w, :].reshape(4 * w, 2 * W)
        return jnp.dot(f, r, preferred_element_type=F32)

    def cube(ns, j0, j1):
        if not len(ns) or j0 >= j1:
            return

        @pl.loop(j0, j1)
        def _(j):
            @pl.loop(0, SUB)
            def _(m):
                acc = total[j, m]
                for n in ns:
                    acc += cubed(n, j, m)
                total[j, m] = acc

    last = NU - 1
    sieve(0)
    pl.semaphore_wait(bar, len(near))
    st1(0)
    for j in range(NCH):
        if j:
            sieve(j)
        own_left(j).start()
    for k in range(2):
        l_send(0, k).start()
    st1(1)

    met = {}
    for t in range(NU + 2):
        s = t - 2
        if t == 1:
            for k in range(2):
                l_send(0, k).wait_recv()
                l_relay(0, k).start()
            for k in range(2):
                l_send(1, k).start()
        if 1 <= t <= NU:
            st3(t - 1, (0,))
        if t == 0:
            st1_wait(0)
            st2(0)
            st2_here(0)
            for n in range(2, NU):
                st1(n)
            st1_wait(1)
            st2_here(1)
            total[...] = jnp.zeros_like(total)
        elif t < NU:
            st2(t)
            if t + 1 < NU:
                st1_wait(t + 1)
                st2_here(t + 1)
        if 1 <= t <= NU:
            st3(t - 1, (1, 2))
            share_first(t - 1)
        if s >= 1:
            sift(s - 1, EARLY if s == 1 else 0)
        if t == 2:
            for k in range(2):
                l_send(1, k).wait_recv()
                l_relay(1, k).start()
        if s < 0:
            continue
        share(s)
        square(s)
        if s == 0 and EARLY:
            sift(0, 0, 1)
        if s >= 1:
            sift_relay(s - 1)
        if s >= 2:
            sift_wait(s - 2)
            ready = [j for j in range(NCH) if all(n <= s for n in range(NU) if UNITS[n][0] == j)]
            cube_up(ready, s - 1, met, cube)
    sift(last)
    sift_wait(last - 1)
    cube_up(list(range(NCH)), last, met, cube)
    sift_relay(last)

    @pl.loop(0, SUB)
    def _(m):
        for k in range(2):
            f_relay(last, m, k).wait_recv()

        @pl.loop(0, NCH)
        def _(j):
            total[j, m] = total[j, m] + cubed(last, j, m)
            csend[j, m] = total[j, m, :, cols(1 - yl)].astype(BF16)
            c_send(j, m).start()

    number_slots()
    for copy in pending:
        copy.wait_send()
    for n in range(NU):
        rc(half(n, core), half(n, 1 - core), ds_.at[n], dr.at[n], other).wait_send()
    for m in range(SUB):
        for k in range(2):
            l_send(m, k).wait_send()
            l_relay(m, k).wait_send()
    for n in range(NU):
        for m in range(SUB):
            s_send(n, m).wait_send()
            for k in range(2):
                f_send(n, m, k).wait_send()
                f_relay(n, m, k).wait_send()

    @pl.loop(0, SUB)
    def _(m):
        @pl.loop(0, NCH)
        def _(j):
            c_send(j, m).wait_recv()
            for i in range(W // B):
                for b in range(BW):
                    mine_ = pl.ds(pl.multiple_of(yl * W + b * B, B), B)
                    rows, cb = slice(i * B, (i + 1) * B), slice(b * B, (b + 1) * B)
                    v = (total[j, m, rows, mine_] + crecv[j, m, rows, cb].astype(F32)) * -2.0
                    blocks[(m * (W // B) + i) * 8 + j * BW + b] = v.astype(BF16)

    r = lax.axis_index("row")

    def slot(s):
        block = blocks[index[s]]
        return jnp.where(valid[s] != 0, block, jnp.zeros_like(block))

    there = dev(x, y + 2, z, core)
    copies = []

    def over(n):
        dx, dc = ACROSS[n]
        at = dev(x + dx, y + 2, z, (core + dc) % 2)[0] * 4
        for k in range(4):
            packed[at + k] = slot(at + k)
        copies.append(rc(packed.at[pl.ds(at, 4)], landed.at[n], as_.at[n], ar.at[n], there))
        copies[-1].start()

    for n in range(FLIGHT):
        over(n)
    along = []
    for n, (dx, dc) in enumerate(ACROSS):
        if (dx, dc) == (0, 0):
            continue
        to = dev(x + dx, y, z, (core + dc) % 2)
        at = to[0] * 4
        for k in range(4):
            packed[at + k] = slot(at + k)
        along.append(rc(packed.at[pl.ds(at, 4)], out.at[pl.ds(r * 4, 4)], as_.at[8 + n], ar.at[8 + n], to))
        along[-1].start()
    for k in range(4):
        out[r * 4 + k] = slot(r * 4 + k)
    for n, (dx, dc) in enumerate(ACROSS):
        to = dev(x + dx, y, z, (core + dc) % 2)
        copies[n].wait_recv()
        if n + FLIGHT < 8:
            over(n + FLIGHT)
        at = out.at[pl.ds(there[0] * 4, 4)]
        if (dx, dc) == (0, 0):
            stay = pltpu.make_async_copy(landed.at[n], at, as_.at[16 + n])
            stay.start()
        else:
            along.append(rc(landed.at[n], at, as_.at[16 + n], ar.at[16 + n], to))
            along[-1].start()

    @pl.loop(0, NCH)
    def _(j):
        @pl.loop(0, SUB)
        def _(m):
            c_send(j, m).wait_send()

    stay.wait()
    for copy in copies:
        copy.wait_send()
    for copy in along:
        copy.wait()


def per_device(u, present, surviving, owners):
    vm = pl.BlockSpec(memory_space=pltpu.VMEM)
    sm = pl.BlockSpec(memory_space=pltpu.SMEM)
    dma = pltpu.SemaphoreType.DMA
    vmem = pltpu.VMEM
    arrived = pl.pallas_call(
        step_kernel,
        out_shape=jax.ShapeDtypeStruct((64, B, B), BF16),
        in_specs=[vm, sm, sm, sm],
        out_specs=vm,
        scratch_shapes=[
            vmem((2, NCH, SUB, W, W), BF16),
            vmem((NCH, NCH, 2, 2, W, 2 * W), BF16),
            vmem((NCH, SUB, W, 4 * W), BF16),
            vmem((NCH, SUB, W, 4 * W), BF16),
            vmem((NCH, SUB, W, W), BF16),
            vmem((SUB, W, 2 * W), F32),
            vmem((NCH, SUB, W, W), BF16),
            vmem((NCH, SUB, W, W), BF16),
            vmem((NCH, SUB, W, W), BF16),
            vmem((NCH, SUB, W, W), BF16),
            vmem((NCH, SUB, W, 2 * W), F32),
            vmem((32, B, B), BF16),
            vmem((64, B, B), BF16),
            vmem((8, 4, B, B), BF16),
            pltpu.SMEM((64,), jnp.int32),
            pltpu.SMEM((64,), jnp.int32),
            dma((NU, 2)), dma((NU, 2)),
            dma((NU, 2, 3)), dma((NU, 2, 3)),
            dma((NU, 4, 2)), dma((NU, 4, 2)),
            dma((NU,)), dma((NU,)), dma((NU, 2)),
            dma((NCH, 3)), dma((NCH, 2)), dma((NCH, 2)), dma((NCH, 2)),
            dma((NU, SUB, 2)), dma((NU, SUB, 2)), dma((NU, SUB, 2)), dma((NU, SUB, 2)),
            dma((NU, SUB)), dma((NU, SUB)), dma((NCH, SUB)), dma((NCH, SUB)),
            dma((24,)), dma((24,)),
        ],
        compiler_params=pltpu.CompilerParams(
            collective_id=0, has_side_effects=True, vmem_limit_bytes=46 * 2**20
        ),
        cost_estimate=pl.CostEstimate(flops=17179869184, bytes_accessed=2 * 2**20, transcendentals=0),
        name="step",
    )(u, present, surviving, owners)
    return arrived.reshape(64, 1, B * B)


def solution(mesh):
    placed = (P("row", "col"), P("row", "col"), P("row", "col"), P("row", "col"))
    return jax.shard_map(
        per_device, mesh=mesh, in_specs=placed, out_specs=P("row", "col", None), check_vma=False
    )
```

```python
import jax
import jax.numpy as jnp
from jax import lax
from jax.experimental import pallas as pl
from jax.experimental.pallas import tpu as pltpu
from jax.sharding import PartitionSpec as P

MESH = pl.DeviceIdType.MESH
B = 128
ROWS = 512
COLS = 1024
NCH = 4
W = COLS // NCH
SUB = ROWS // W
HS = SUB // 2
UNITS = ((0, 0, 256), (1, 0, 256), (2, 0, 256), (3, 0, 128), (3, 128, 128))
NU = len(UNITS)
FLIGHT = 3
EARLY = 1
BW = W // B
ACROSS = ((2, 0), (2, 1), (1, 0), (3, 1), (3, 0), (1, 1), (0, 1), (0, 0))
F32 = jnp.float32
BF16 = jnp.bfloat16


def coords():
    r = lax.axis_index("row")
    c = lax.axis_index("col")
    return (r // 2) % 4, (r // 8) * 2 + c % 2, c // 2, r % 2


def dev(x, y, z, core):
    x = (x + 8) % 4
    y = (y + 8) % 4
    z = (z + 8) % 4
    return ((y // 2) * 8 + x * 2 + core, z * 2 + y % 2)


def cube_up(chunks, upto, met, cube):
    groups = {}
    for j in chunks:
        groups.setdefault(met.get(j, 0), []).append(j)
        met[j] = upto
    for first, js in groups.items():
        cube(list(range(first, upto)), js[0], js[-1] + 1)


def cols(at, width=W):
    return pl.ds(pl.multiple_of(at * W, W), width)


def step_kernel(
    u, table, out,
    own, right, left, fleft, fown, sums, ssend, srecv, csend, crecv, total, blocks, packed, landed, index, valid,
    s1s, s1r, s2s, s2r, s3s, s3r, ds_, dr, loc, ls, lr, lrs, lrr, fs, fr, frs, frr, xs, xr, cs, cr, as_, ar,
):
    x, y, z, core = coords()
    yl = y % 2
    q = (x + y) % 2
    bar = pltpu.get_barrier_semaphore()
    xp, xm = dev(x + 1, y, z, core), dev(x - 1, y, z, core)
    yp, ym, yy = dev(x, y + 1, z, core), dev(x, y - 1, z, core), dev(x, y + 2, z, core)
    zp, zm = dev(x, y, z + 1, core), dev(x, y, z - 1, core)
    other = dev(x, y, z, 1 - core)
    partner = dev(x, (y // 2) * 2 + 1 - yl, z, core)
    near = [yp, ym, yy, zp, zm]
    near += [dev(x + dx, y, z, (core + dc) % 2) for dx, dc in ACROSS if (dx, dc) != (0, 0)]
    for d in near:
        pl.semaphore_signal(bar, inc=1, device_id=d, device_id_type=MESH)

    def rc(src, dst, ssem, rsem, to):
        return pltpu.make_async_remote_copy(
            src_ref=src, dst_ref=dst, send_sem=ssem, recv_sem=rsem, device_id=to, device_id_type=MESH
        )

    pending = []

    def go(copy):
        copy.start()
        pending.append(copy)

    def piece(n, xs_, ys_, h):
        xs_ = (xs_ + 8) % 4
        ys_ = (ys_ + 8) % 4
        k = core * (NCH // 2) + h * HS
        j, c, w = UNITS[n]
        return right.at[j, pl.ds(k, HS), ys_ // 2, xs_ // 2, :, pl.ds(pl.multiple_of((ys_ % 2) * W + c, B), w)]

    def number_slots():
        at = []
        owned = [table[b // 8, b % 8] >> 2 for b in range(32)]
        for b in range(32):
            o = owned[b]
            rank = jnp.int32(0)
            for e in range(b):
                rank += (owned[e] == o).astype(jnp.int32)
            at.append(o * 4 + rank)

        @pl.loop(0, 64)
        def _(n):
            which, found = jnp.int32(0), jnp.int32(0)
            for b in range(32):
                hit = at[b] == n
                which = jnp.where(hit, b, which)
                found = jnp.where(hit, 1, found)
            index[n] = which
            valid[n] = found

    def sieve(j):
        for i in range(4):
            for b in range(BW):
                keep = (table[i, j * BW + b] & 1) != 0
                block = u[i * B:(i + 1) * B, j * W + b * B:j * W + (b + 1) * B]
                r0 = (i * B) % W
                kept = jnp.where(keep, block, jnp.zeros_like(block))
                own[0, j, (i * B) // W, r0:r0 + B, b * B:(b + 1) * B] = kept

    def part(h):
        return pl.ds(h * HS, HS)

    def shift(h):
        return 1 if h else -1

    def mine(g, n, h):
        j, c, w = UNITS[n]
        return own.at[g, j, part(h), :, pl.ds(c, w)]

    def st1(n):
        for h in range(2):
            go(rc(mine(0, n, h), mine(1, n, h), s1s.at[n, h], s1r.at[n, h], xm if h else xp))

    def along_x(j, h, d, src):
        at = piece(j, x + q * shift(h), y + d, h)
        to = dev(x + shift(h) * (1 - 2 * q), y, z, core)
        go(rc(at if src is None else src, at, s3s.at[j, d % 4, h], s3r.at[j, d % 4, h], to))

    def st1_wait(n):
        for h in range(2):
            rc(mine(0, n, h), mine(1, n, h), s1s.at[n, h], s1r.at[n, h], xp).wait_recv()

    def st2(n):
        for h in range(2):
            wrong = mine(1 - q, n, h)
            fine = mine(q, n, h)
            wx = x + (1 - q) * shift(h)
            fx = x + q * shift(h)
            go(rc(wrong, piece(n, wx, y, h), s2s.at[n, h, 0], s2r.at[n, h, 0], yp))
            go(rc(wrong, piece(n, wx, y, h), s2s.at[n, h, 1], s2r.at[n, h, 1], ym))
            go(rc(fine, piece(n, fx, y, h), s2s.at[n, h, 2], s2r.at[n, h, 2], yy))

    def st2_here(n):
        for h in range(2):
            fine = mine(q, n, h)
            along_x(n, h, 0, fine)
            pltpu.make_async_copy(fine, piece(n, x + q * shift(h), y, h), loc.at[n, h]).start()

    def hand_over(n, xs_, h):
        j, c, w = UNITS[n]
        k = core * (NCH // 2) + h * HS
        for c0, wide in ((0, 2 * W),) if w == W else ((c, w), (W + c, w)):
            at = right.at[j, pl.ds(k, HS), :, ((xs_ + 8) % 4) // 2, :, pl.ds(c0, wide)]
            rc(at, at, ds_.at[n], dr.at[n], other).start()

    def st3(j, kinds):
        for kind in kinds:
            for h in range(2):
                d = (-1, 1, 2)[kind]
                at = piece(j, x + q * shift(h), y + d, h)
                rc(at, at, s2s.at[j, h, kind], s2r.at[j, h, kind], yp).wait_recv()
                along_x(j, h, d, None)

    def share_first(j):
        for h in range(2):
            at = mine(q, j, h)
            pltpu.make_async_copy(at, piece(j, x + q * shift(h), y, h), loc.at[j, h]).wait()
            hand_over(j, x + q * shift(h), h)

    def share(j):
        for h in range(2):
            for d in (0, -1, 1, 2):
                at = piece(j, x + q * shift(h) + 2, y + d, h)
                rc(at, at, s3s.at[j, d % 4, h], s3r.at[j, d % 4, h], xp).wait_recv()
            hand_over(j, x + q * shift(h) + 2, h)

    def half(n, core_):
        j, c, w = UNITS[n]
        k = pl.ds(core_ * (NCH // 2), NCH // 2)
        return right.at[j, k, :, :, :, pl.ds(0, 2 * w)]

    def l_send(m, k):
        at = left.at[:, m, :, cols(z)]
        return rc(own.at[0, :, m], at, ls.at[m, k], lr.at[m, k], (zp, zm)[k])

    def l_relay(m, k):
        on = left.at[:, m, pl.ds(k * (W // 2), W // 2), cols((z + (3, 1)[k]) % 4)]
        return rc(on, on, lrs.at[m, k], lrr.at[m, k], (zp, zm)[k])

    def f_send(n, m, k):
        j, c, w = UNITS[n]
        at = fleft.at[j, m, :, pl.ds(pl.multiple_of(z * W + c, B), w)]
        return rc(fown.at[j, m, :, pl.ds(c, w)], at, fs.at[n, m, k], fr.at[n, m, k], (zp, zm)[k])

    def f_relay(n, m, k):
        j, c, w = UNITS[n]
        lane = pl.multiple_of(((z + (3, 1)[k]) % 4) * W + c, B)
        on = fleft.at[j, m, pl.ds(k * (W // 2), W // 2), pl.ds(lane, w)]
        return rc(on, on, frs.at[n, m, k], frr.at[n, m, k], (zp, zm)[k])

    def s_send(n, m):
        j, c, w = UNITS[n]
        at = pl.ds(c, w)
        return rc(ssend.at[j, m, :, at], srecv.at[j, m, :, at], xs.at[n, m], xr.at[n, m], partner)

    def c_send(j, m):
        return rc(csend.at[j, m], crecv.at[j, m], cs.at[j, m], cr.at[j, m], partner)

    def own_left(j):
        return pltpu.make_async_copy(own.at[0, j], left.at[j, :, :, cols(z)], ls.at[j, 2])

    def square(n):
        j, c, w = UNITS[n]
        if n == 0:
            for i in range(NCH):
                own_left(i).wait()
        rc(half(n, core), half(n, 1 - core), ds_.at[n], dr.at[n], other).wait_recv()

        def rows(m):
            acc = None
            for k in range(NCH):
                if w == W:
                    r = right[j, k].reshape(4 * W, 2 * W)
                else:
                    r = [right[j, k, :, :, :, c0:c0 + w].reshape(4 * W, w) for c0 in (c, W + c)]
                    r = jnp.concatenate(r, axis=1)
                d = jnp.dot(left[k, m], r, preferred_element_type=F32)
                acc = d if acc is None else acc + d
            sums[m, :, 0:2 * w] = acc
            ssend[j, m, :, c:c + w] = sums[m, :, pl.ds(pl.multiple_of((1 - yl) * w, B), w)].astype(BF16)
            s_send(n, m).start()

        if n:
            pl.loop(0, SUB)(rows)
        else:
            for m in range(SUB):
                for k in range(2):
                    l_relay(m, k).wait_recv()
                rows(m)

    def sift(n, m0=0, m1=SUB):
        j, c, w = UNITS[n]

        @pl.loop(m0, m1)
        def _(m):
            s_send(n, m).wait_recv()
            for i in range(W // B):
                rows = slice(i * B, (i + 1) * B)
                for b in range(c // B, (c + w) // B):
                    keep = ((table[m * (W // B) + i, j * BW + b] >> 1) & 1).astype(F32)
                    at = pl.ds(pl.multiple_of(yl * w + b * B - c, B), B)
                    mine_ = pl.ds(pl.multiple_of(yl * W + b * B, B), B)
                    cb = slice(b * B, (b + 1) * B)
                    f = (sums[m, rows, at] + srecv[j, m, rows, cb].astype(F32)) * keep
                    fb = f.astype(BF16)
                    fown[j, m, rows, cb] = fb
                    fleft[j, m, rows, pl.ds(pl.multiple_of(z * W + b * B, B), B)] = fb
                    total[j, m, rows, mine_] = total[j, m, rows, mine_] + f * -1.5
            for k in range(2):
                f_send(n, m, k).start()

    def sift_relay(j):
        @pl.loop(0, SUB)
        def _(m):
            for k in range(2):
                f_send(j, m, k).wait_recv()
                f_relay(j, m, k).start()

    def sift_wait(j):
        @pl.loop(0, SUB)
        def _(m):
            for k in range(2):
                f_relay(j, m, k).wait_recv()

    def cubed(n, j, m):
        k, c, w = UNITS[n]
        if w == W:
            return jnp.dot(fleft[k, m], right[j, k].reshape(4 * W, 2 * W), preferred_element_type=F32)
        f = jnp.concatenate([fleft[k, m, :, i * W + c:i * W + c + w] for i in range(4)], axis=1)
        r = right[j, k, :, :, c:c + w, :].reshape(4 * w, 2 * W)
        return jnp.dot(f, r, preferred_element_type=F32)

    def cube(ns, j0, j1):
        if not len(ns) or j0 >= j1:
            return

        @pl.loop(j0, j1)
        def _(j):
            @pl.loop(0, SUB)
            def _(m):
                acc = total[j, m]
                for n in ns:
                    acc += cubed(n, j, m)
                total[j, m] = acc

    last = NU - 1
    sieve(0)
    pl.semaphore_wait(bar, len(near))
    st1(0)
    for j in range(NCH):
        if j:
            sieve(j)
        own_left(j).start()
    for k in range(2):
        l_send(0, k).start()
    st1(1)

    met = {}
    for t in range(NU + 2):
        s = t - 2
        if t == 1:
            for k in range(2):
                l_send(0, k).wait_recv()
                l_relay(0, k).start()
            for k in range(2):
                l_send(1, k).start()
        if 1 <= t <= NU:
            st3(t - 1, (0,))
        if t == 0:
            st1_wait(0)
            st2(0)
            st2_here(0)
            for n in range(2, NU):
                st1(n)
            st1_wait(1)
            st2_here(1)
            total[...] = jnp.zeros_like(total)
        elif t < NU:
            st2(t)
            if t + 1 < NU:
                st1_wait(t + 1)
                st2_here(t + 1)
        if 1 <= t <= NU:
            st3(t - 1, (1, 2))
            share_first(t - 1)
        if s >= 1:
            sift(s - 1, EARLY if s == 1 else 0)
        if t == 2:
            for k in range(2):
                l_send(1, k).wait_recv()
                l_relay(1, k).start()
        if s < 0:
            continue
        share(s)
        square(s)
        if s == 0 and EARLY:
            sift(0, 0, 1)
        if s >= 1:
            sift_relay(s - 1)
        if s >= 2:
            sift_wait(s - 2)
            ready = [j for j in range(NCH) if all(n <= s for n in range(NU) if UNITS[n][0] == j)]
            cube_up(ready, s - 1, met, cube)
    sift(last)
    sift_wait(last - 1)
    cube_up(list(range(NCH)), last, met, cube)
    sift_relay(last)

    @pl.loop(0, SUB)
    def _(m):
        for k in range(2):
            f_relay(last, m, k).wait_recv()

        @pl.loop(0, NCH)
        def _(j):
            total[j, m] = total[j, m] + cubed(last, j, m)
            csend[j, m] = total[j, m, :, cols(1 - yl)].astype(BF16)
            c_send(j, m).start()

    number_slots()
    for copy in pending:
        copy.wait_send()
    for n in range(NU):
        rc(half(n, core), half(n, 1 - core), ds_.at[n], dr.at[n], other).wait_send()
    for m in range(SUB):
        for k in range(2):
            l_send(m, k).wait_send()
            l_relay(m, k).wait_send()
    for n in range(NU):
        for m in range(SUB):
            s_send(n, m).wait_send()
            for k in range(2):
                f_send(n, m, k).wait_send()
                f_relay(n, m, k).wait_send()

    @pl.loop(0, SUB)
    def _(m):
        @pl.loop(0, NCH)
        def _(j):
            c_send(j, m).wait_recv()
            for i in range(W // B):
                for b in range(BW):
                    mine_ = pl.ds(pl.multiple_of(yl * W + b * B, B), B)
                    rows, cb = slice(i * B, (i + 1) * B), slice(b * B, (b + 1) * B)
                    v = (total[j, m, rows, mine_] + crecv[j, m, rows, cb].astype(F32)) * -2.0
                    blocks[(m * (W // B) + i) * 8 + j * BW + b] = v.astype(BF16)

    r = lax.axis_index("row")

    def slot(s):
        block = blocks[index[s]]
        return jnp.where(valid[s] != 0, block, jnp.zeros_like(block))

    there = dev(x, y + 2, z, core)
    copies = []

    def over(n):
        dx, dc = ACROSS[n]
        at = dev(x + dx, y + 2, z, (core + dc) % 2)[0] * 4
        for k in range(4):
            packed[at + k] = slot(at + k)
        copies.append(rc(packed.at[pl.ds(at, 4)], landed.at[n], as_.at[n], ar.at[n], there))
        copies[-1].start()

    for n in range(FLIGHT):
        over(n)
    along = []
    for n, (dx, dc) in enumerate(ACROSS):
        if (dx, dc) == (0, 0):
            continue
        to = dev(x + dx, y, z, (core + dc) % 2)
        at = to[0] * 4
        for k in range(4):
            packed[at + k] = slot(at + k)
        along.append(rc(packed.at[pl.ds(at, 4)], out.at[pl.ds(r * 4, 4)], as_.at[8 + n], ar.at[8 + n], to))
        along[-1].start()
    for k in range(4):
        out[r * 4 + k] = slot(r * 4 + k)
    for n, (dx, dc) in enumerate(ACROSS):
        to = dev(x + dx, y, z, (core + dc) % 2)
        copies[n].wait_recv()
        if n + FLIGHT < 8:
            over(n + FLIGHT)
        at = out.at[pl.ds(there[0] * 4, 4)]
        if (dx, dc) == (0, 0):
            stay = pltpu.make_async_copy(landed.at[n], at, as_.at[16 + n])
            stay.start()
        else:
            along.append(rc(landed.at[n], at, as_.at[16 + n], ar.at[16 + n], to))
            along[-1].start()

    @pl.loop(0, NCH)
    def _(j):
        @pl.loop(0, SUB)
        def _(m):
            c_send(j, m).wait_send()

    stay.wait()
    for copy in copies:
        copy.wait_send()
    for copy in along:
        copy.wait()


def per_device(u, present, surviving, owners):
    vm = pl.BlockSpec(memory_space=pltpu.VMEM)
    sm = pl.BlockSpec(memory_space=pltpu.SMEM)
    dma = pltpu.SemaphoreType.DMA
    vmem = pltpu.VMEM
    arrived = pl.pallas_call(
        step_kernel,
        out_shape=jax.ShapeDtypeStruct((64, B, B), BF16),
        in_specs=[vm, sm],
        out_specs=vm,
        scratch_shapes=[
            vmem((2, NCH, SUB, W, W), BF16),
            vmem((NCH, NCH, 2, 2, W, 2 * W), BF16),
            vmem((NCH, SUB, W, 4 * W), BF16),
            vmem((NCH, SUB, W, 4 * W), BF16),
            vmem((NCH, SUB, W, W), BF16),
            vmem((SUB, W, 2 * W), F32),
            vmem((NCH, SUB, W, W), BF16),
            vmem((NCH, SUB, W, W), BF16),
            vmem((NCH, SUB, W, W), BF16),
            vmem((NCH, SUB, W, W), BF16),
            vmem((NCH, SUB, W, 2 * W), F32),
            vmem((32, B, B), BF16),
            vmem((64, B, B), BF16),
            vmem((8, 4, B, B), BF16),
            pltpu.SMEM((64,), jnp.int32),
            pltpu.SMEM((64,), jnp.int32),
            dma((NU, 2)), dma((NU, 2)),
            dma((NU, 2, 3)), dma((NU, 2, 3)),
            dma((NU, 4, 2)), dma((NU, 4, 2)),
            dma((NU,)), dma((NU,)), dma((NU, 2)),
            dma((NCH, 3)), dma((NCH, 2)), dma((NCH, 2)), dma((NCH, 2)),
            dma((NU, SUB, 2)), dma((NU, SUB, 2)), dma((NU, SUB, 2)), dma((NU, SUB, 2)),
            dma((NU, SUB)), dma((NU, SUB)), dma((NCH, SUB)), dma((NCH, SUB)),
            dma((24,)), dma((24,)),
        ],
        compiler_params=pltpu.CompilerParams(
            collective_id=0, has_side_effects=True, vmem_limit_bytes=46 * 2**20
        ),
        cost_estimate=pl.CostEstimate(flops=17179869184, bytes_accessed=2 * 2**20, transcendentals=0),
        name="step",
    )(u, present + 2 * surviving + 4 * owners)
    return arrived.reshape(64, 1, B * B)


def solution(mesh):
    placed = (P("row", "col"), P("row", "col"), P("row", "col"), P("row", "col"))
    return jax.shard_map(
        per_device, mesh=mesh, in_specs=placed, out_specs=P("row", "col", None), check_vma=False
    )
```
